512 devices in a mesh: pipe: 16 (over z_hi, y, core), expert: 32 (over z_lo, x).
Axes of the slice: x: 4, y: 4, z: 16 (z_hi: 2, z_lo: 8; z = z_hi * 8 + z_lo), core: 2. Of those that a mesh axis runs over, the one named last changes fastest.
Arguments:
- act_down: bfloat16 [16, 512, 3584], P('pipe', 'expert'), may hold values from -6 to 6
- act_up: bfloat16 [16, 512, 3584], P('pipe', 'expert'), may hold values from -6 to 6
- routes_down: int32 [16, 512, 2], P('pipe', 'expert'), may hold values from 0 to 3, all different within a row; in each aligned block of 16 rows (0 to 15, 16 to 31, ..., all dimensions but the last counted through in order) at most 12 rows name the same one
- routes_up: int32 [16, 512, 2], P('pipe', 'expert'), may hold values from 0 to 3, all different within a row; in each aligned block of 16 rows (0 to 15, 16 to 31, ..., all dimensions but the last counted through in order) at most 12 rows name the same one
- norm_gain: float32 [16, 3584], P('pipe'), may hold values from 0.5 to 1.5
- router_w: bfloat16 [16, 3584, 4], P('pipe'), may hold values from -0.09375 to 0.09375
- w_gate: bfloat16 [16, 3584, 4096], P('pipe', None, 'expert'), may hold values from -0.09375 to 0.09375
- w_up: bfloat16 [16, 3584, 4096], P('pipe', None, 'expert'), may hold values from -0.09375 to 0.09375
- w_down: bfloat16 [16, 4096, 3584], P('pipe', 'expert'), may hold values from -0.1875 to 0.1875
Outputs:
- next_down: bfloat16 [16, 512, 3584], P('pipe', 'expert')
- next_up: bfloat16 [16, 512, 3584], P('pipe', 'expert')
The draws below stay inside these ranges and needn't reach their ends.
Inputs may be any that keep to these rules, and one draw needn't show every extreme that they name: `routes_down`: each token names 2 different experts. In each aligned block of 16 tokens (the tokens of one device) no expert is named by more than 12 tokens, a bound that some block reaches. `routes_up`: as for routes_down.
All inputs are finite; a program needn't handle non-finite values.
Results may differ from the reference program's by a relative error of at most 0.006.
Values may be sent and summed in bfloat16 or wider, within the bound.
No kernel may reach another device: no remote copies, remote signals or barrier semaphores. Data moves between devices by JAX's collectives and lax.ppermute only.
A program may use at most 64 MiB of HBM per device.

```python
import math
import jax
import jax.numpy as jnp
import numpy as np
from jax import lax

D = 3584
FF = 1024
EXPERTS = 4
TOPK = 2
MB_DEV = 16
CAP = 12
TOK = 512
GROUP = 8
FF_DEV = 128
N_PIPE = 16
N_EXPERT = 32


def steps_of(key, extent, split, smallest, largest):
    factor_of, own = 1.0, jax.random.fold_in(key, 6)
    for position, blocks in split:
        steps = jnp.exp(jax.random.uniform(jax.random.fold_in(own, position), (blocks,), jnp.float32, smallest / len(split), largest / len(split)))
        factor_of = factor_of * jnp.repeat(steps, extent[position] // blocks).reshape([-1 if axis == position else 1 for axis in range(len(extent))])
    return factor_of


def deal_out(own_key, own, number, rows, number_of, top, most, slope):
    order = jax.random.permutation(own_key, number_of)
    packed, common = shares(number_of, rows * top, most, slope, True), shares(number_of, rows * top, most, slope, False)
    places = jnp.arange(number_of)

    def named(tallies, rotation):
        used = int((tallies > 0).sum())
        fixed = max(1, used // 4)
        shifted = fixed + (places - fixed + rotation * (used - fixed)) % max(1, number_of - fixed)
        return jnp.zeros((number_of,), jnp.int32).at[order[jnp.where(places < fixed, places, shifted)]].set(jnp.asarray(tallies, jnp.int32))

    tallies = jnp.where(number % 4 == 0, named(packed, number // 4), named(common, number - number // 4 - 1))
    mixed = jax.random.permutation(jax.random.fold_in(own, 3), number_of)
    giver, sink = mixed[0:number_of // 2 * 2:2], mixed[1:number_of // 2 * 2:2]
    margin = jnp.minimum(tallies[giver] - 1, most - tallies[sink]) // 2
    margin = jnp.where((giver == order[0]) | (sink == order[0]) | (tallies[sink] == 0), 0, jnp.maximum(margin, 0))
    shifted = jax.random.randint(jax.random.fold_in(own, 4), (number_of // 2,), 0, 1 << 20) % (margin + 1)
    tallies = tallies.at[giver].add(-shifted).at[sink].add(shifted)
    labels = jnp.searchsorted(jnp.cumsum(tallies), jnp.arange(rows * top), side="right").astype(jnp.int32)
    grid = labels.reshape(top, rows).T
    grid = grid[jax.random.permutation(jax.random.fold_in(own, 1), rows)]
    rotation = jax.random.randint(jax.random.fold_in(own, 2), (rows, 1), 0, top)
    return jnp.take_along_axis(grid, (jnp.arange(top)[None, :] + rotation) % top, axis=1)


def shares(number_of, total, most, skew, full):
    weights = [(1 << 20) // math.isqrt(grade ** skew) + 1 for grade in range(1, number_of + 1)]
    largest = most if full else min(most, max(-(-total // number_of), total * weights[0] // sum(weights)))
    least = 1 if total - largest >= number_of - 1 else 0
    holding, surplus = [largest] + [least] * (number_of - 1), total - largest - least * (number_of - 1)
    while surplus > 0:
        movable = [i for i in range(1, number_of) if holding[i] < largest] or [i for i in range(1, number_of) if holding[i] < most]
        mass, left = sum([weights[i] for i in movable]), surplus
        for i in movable:
            addition = min(most - holding[i], max(1, left * weights[i] // mass), surplus)
            holding[i] = holding[i] + addition
            surplus = surplus - addition
    return np.array(holding)


def normal_values(own_key, shape, deviation, reach, cuts=(), held_as=jnp.bfloat16):
    loudness = steps_of(own_key, shape, cuts, -0.22, 0.18) if cuts else 1.0
    drawn = jax.random.normal(own_key, shape, jnp.float32) * deviation * loudness
    return jnp.minimum(jnp.maximum(drawn, -reach), reach).astype(held_as)


def setup_inputs(seed: int = 0) -> dict:
    streams_of = jax.random.split(jax.random.key(seed), 10)
    act_down = normal_values(streams_of[0], (N_PIPE, TOK, D), 1.0, 6.0, ((0, 16), (1, 32)))
    act_up = normal_values(streams_of[1], (N_PIPE, TOK, D), 1.0, 6.0, ((0, 16), (1, 32)))
    routes_down_keys = jax.random.split(jax.random.fold_in(streams_of[2], 1), N_PIPE * TOK // MB_DEV)
    routes_down_turns = jax.random.permutation(jax.random.fold_in(streams_of[2], 3), N_PIPE * TOK // MB_DEV)
    routes_down = jax.vmap(lambda own, number: deal_out(jax.random.fold_in(streams_of[2], 2), own, number, MB_DEV, EXPERTS, TOPK, CAP, 0))(routes_down_keys, routes_down_turns).reshape((N_PIPE, TOK, TOPK))
    routes_up_keys = jax.random.split(jax.random.fold_in(streams_of[3], 1), N_PIPE * TOK // MB_DEV)
    routes_up_turns = jax.random.permutation(jax.random.fold_in(streams_of[3], 3), N_PIPE * TOK // MB_DEV)
    routes_up = jax.vmap(lambda own, number: deal_out(jax.random.fold_in(streams_of[3], 2), own, number, MB_DEV, EXPERTS, TOPK, CAP, 0))(routes_up_keys, routes_up_turns).reshape((N_PIPE, TOK, TOPK))
    norm_gain = jnp.clip(1.0 + 0.1 * jax.random.normal(streams_of[4], (N_PIPE, D), jnp.float32), 0.5, 1.5)
    router_w = normal_values(streams_of[5], (N_PIPE, D, EXPERTS), D ** -0.5, 0.09375, ((0, 16),))
    w_gate = normal_values(streams_of[6], (N_PIPE, D, EXPERTS * FF), D ** -0.5, 0.09375, ((0, 16), (2, 32)))
    w_up = normal_values(streams_of[7], (N_PIPE, D, EXPERTS * FF), D ** -0.5, 0.09375, ((0, 16), (2, 32)))
    w_down = normal_values(streams_of[8], (N_PIPE, EXPERTS * FF, D), FF ** -0.5, 0.1875, ((0, 16), (1, 32)))
    return dict(act_down=act_down, act_up=act_up, routes_down=routes_down, routes_up=routes_up, norm_gain=norm_gain, router_w=router_w, w_gate=w_gate, w_up=w_up, w_down=w_down)


route_scale = 2.5

def section_layer(x, gain, router, gate_cols, up_cols, down_rows, routes):
    xf = x.astype(jnp.float32)
    mean_sq = lax.optimization_barrier(jnp.mean(xf * xf, axis=-1, keepdims=True))
    normed = (xf * lax.rsqrt(mean_sq + 1e-06) * gain).astype(jnp.bfloat16)
    logits = jnp.dot(normed, router, preferred_element_type=jnp.float32)
    affinity = jax.nn.sigmoid(logits)
    picked = jnp.take_along_axis(affinity, routes, axis=1)
    weights = picked / lax.optimization_barrier(jnp.sum(picked, axis=1, keepdims=True)) * route_scale
    total = jnp.zeros(xf.shape, jnp.float32)
    limit = min(N_EXPERT * CAP, x.shape[0])
    for expert in range(EXPERTS):
        hits = routes == expert
        share = lax.optimization_barrier(jnp.sum(jnp.where(hits, weights, jnp.zeros_like(weights)), axis=1))
        keys = jnp.where(jnp.any(hits, axis=1), 0, 1).astype(jnp.int32)
        order = jnp.argsort(keys, stable=True)[:limit].astype(jnp.int32)
        rows = normed[order]
        gate = jnp.dot(rows, gate_cols[:, expert * FF:(expert + 1) * FF], preferred_element_type=jnp.float32)
        upper = jnp.dot(rows, up_cols[:, expert * FF:(expert + 1) * FF], preferred_element_type=jnp.float32)
        hidden = (jax.nn.silu(gate) * upper).astype(jnp.bfloat16)
        blocks = hidden.astype(jnp.float32).reshape(limit, GROUP, FF_DEV)
        down_part = down_rows[expert * FF:(expert + 1) * FF].astype(jnp.float32).reshape(GROUP, FF_DEV, D)
        pieces = jnp.einsum('rgf,gfd->rgd', blocks, down_part, precision=lax.Precision.HIGHEST)
        pieces = lax.optimization_barrier(pieces.astype(jnp.bfloat16)).astype(jnp.float32)
        output = lax.optimization_barrier(jnp.sum(pieces, axis=1))
        total = total.at[order].add(output * share[order][:, None])
    return (xf + total).astype(jnp.bfloat16)

def reference(act_down, act_up, routes_down, routes_up, norm_gain, router_w, w_gate, w_up, w_down):
    outs_down = []
    outs_up = []
    for section in range(N_PIPE):
        outs_down.append(section_layer(act_down[section], norm_gain[section], router_w[section], w_gate[section], w_up[section], w_down[section], routes_down[section]))
        outs_up.append(section_layer(act_up[section], norm_gain[section], router_w[section], w_gate[section], w_up[section], w_down[section], routes_up[section]))
    next_down = jnp.roll(jnp.stack(outs_down), 1, axis=0)
    next_up = jnp.roll(jnp.stack(outs_up), -1, axis=0)
    return (next_down, next_up)
```

```python
import jax
import jax.numpy as jnp
from jax import lax
from jax.sharding import PartitionSpec as P

CAP = 12
ALONG_X = 4
UNITS = 2

route_scale = 2.5


def index_of(z, x):
    return z * ALONG_X + x


def places():
    columns = lax.axis_size("expert") // ALONG_X
    return [(z, x) for z in range(columns) for x in range(ALONG_X)]


def along_x(block, step):
    route = [(index_of(z, x), index_of(z, (x + step) % ALONG_X)) for z, x in places()]
    return lax.ppermute(block, "expert", route)


def along_z(block, step):
    columns = lax.axis_size("expert") // ALONG_X
    route = [(index_of(z, x), index_of((z + step) % columns, x)) for z, x in places()]
    return lax.ppermute(block, "expert", route)


def swapped(block):
    route = [(index_of(z, x), index_of(z ^ 1, x)) for z, x in places()]
    return lax.ppermute(block, "expert", route)


def to_section(block, section_step, z_step):
    sections, devices = lax.axis_size("pipe"), lax.axis_size("expert")
    columns = devices // ALONG_X
    route = [
        (
            s * devices + index_of(z, x),
            (s + section_step) % sections * devices + index_of((z + z_step) % columns, x),
        )
        for s in range(sections)
        for z, x in places()
    ]
    return lax.ppermute(block, ("pipe", "expert"), route)


def gather_x(block):
    half = block.shape[0] // 2
    left = along_x(block, 1)
    right = along_x(block, -1)
    far_top = along_x(left[:half], 1)
    far_bottom = along_x(right[half:], -1)
    return left, right, far_top, far_bottom


def prepare(x, routes, gain, router, group):
    xf = x.astype(jnp.float32)
    mean_sq = jnp.mean(xf * xf, axis=-1, keepdims=True)
    normed = (xf * lax.rsqrt(mean_sq + 1e-06) * gain).astype(jnp.bfloat16)
    logits = jnp.dot(normed, router, preferred_element_type=jnp.float32)
    affinity = jax.nn.sigmoid(logits)
    experts_n = router.shape[1]
    hits = routes[:, :, None] == jnp.arange(experts_n, dtype=jnp.int32)
    picked = jnp.sum(jnp.where(hits, affinity[:, None, :], 0.0), axis=2)
    weights = picked / jnp.sum(picked, axis=1, keepdims=True) * route_scale
    named = jnp.any(hits, axis=1)
    share = jnp.sum(jnp.where(hits, weights[:, :, None], 0.0), axis=1)
    count = named.astype(jnp.int32)
    before = jnp.cumsum(count, axis=0) - count
    turn = jnp.mod(jnp.arange(experts_n, dtype=jnp.int32) + group, experts_n)
    rolled = turn[:, None] == jnp.arange(experts_n, dtype=jnp.int32)
    pick = lambda v: jnp.sum(jnp.where(rolled, v[:, None, :], jnp.zeros((), v.dtype)), axis=2)
    slot = jnp.where(pick(count) > 0, pick(before), -1)
    chosen = slot[:, :, None] == jnp.arange(CAP, dtype=jnp.int32)
    combine = jnp.where(chosen, pick(share)[:, :, None], 0.0)
    return normed, chosen, combine


def on_device(act_down, act_up, routes_down, routes_up, norm_gain, router_w, w_gate, w_up, w_down):
    experts_n = router_w.shape[2]
    width = act_down.shape[2]
    rows_n = act_down.shape[1]
    part = width // UNITS
    piece = part // 2
    gain = norm_gain[0]
    router = router_w[0]
    both_cols = jnp.concatenate([w_gate[0], w_up[0]], axis=1)
    down_rows = w_down[0]
    hidden_n = down_rows.shape[0]
    group = lax.axis_index("expert") // ALONG_X // 2

    cols_all = (both_cols,) + gather_x(both_cols)
    down_all = []
    for unit in range(UNITS):
        mine = down_rows[:, unit * part:(unit + 1) * part]
        down_all.append((mine,) + gather_x(mine))

    normed_d, chosen_d, combine_d = prepare(act_down[0], routes_down[0], gain, router, group)
    normed_u, chosen_u, combine_u = prepare(act_up[0], routes_up[0], gain, router, group)
    select = jnp.stack(
        [jnp.pad(chosen_d, ((0, rows_n), (0, 0), (0, 0))), jnp.pad(chosen_u, ((rows_n, 0), (0, 0), (0, 0)))],
        axis=2,
    ).reshape(2 * rows_n, experts_n * 2 * CAP)
    packed = lax.dot_general(
        select.astype(jnp.bfloat16),
        jnp.concatenate([normed_d, normed_u], axis=0),
        (((0,), (0,)), ((), ())),
        preferred_element_type=jnp.float32,
    ).astype(jnp.bfloat16)
    chunk = 2 * CAP
    near = [packed[:chunk]] + [
        along_z(packed[s * chunk:(s + 1) * chunk], 2 * s) for s in range(1, experts_n)
    ]
    mine = jnp.concatenate(near, axis=0)
    rows = jnp.concatenate([mine, swapped(mine)], axis=0)

    def spread(combine):
        blocks = jnp.zeros((2, rows_n, experts_n, 2, CAP), jnp.float32)
        blocks = blocks.at[0, :, :, 0, :].set(combine).at[1, :, :, 1, :].set(combine)
        return blocks.reshape(2 * rows_n, experts_n * chunk)

    res_down = to_section(act_down[0], 1, 0)
    res_up = to_section(act_up[0], -1, 0)
    mix_down = to_section(spread(combine_d), 1, 0)
    mix_up = to_section(spread(combine_u), -1, 0)

    dot = lambda a, b: jnp.dot(a, b, preferred_element_type=jnp.float32)
    act = lambda joined: (jax.nn.silu(joined[:, :hidden_n]) * joined[:, hidden_n:]).astype(jnp.bfloat16)
    own, left, right, far_top, far_bottom = cols_all
    half = far_top.shape[0]
    hidden = [act(dot(rows, own)), act(dot(rows, left)), act(dot(rows, right))]
    hidden.append(act(dot(rows[:, :half], far_top) + dot(rows[:, half:], far_bottom)))
    hidden = jnp.concatenate(hidden, axis=1)

    back_down, back_up = [], []
    for unit in range(UNITS):
        total = dot(hidden, jnp.concatenate(down_all[unit], axis=0))
        held = rows.shape[0] // 2
        theirs = swapped(total[held:].astype(jnp.bfloat16))
        summed = (total[:held] + theirs.astype(jnp.float32)).astype(jnp.bfloat16)
        summed = summed.reshape(experts_n, 2, CAP, 2, piece).transpose(0, 1, 3, 2, 4)
        summed = summed.reshape(experts_n, 2, chunk, piece)
        back_down.append(jnp.concatenate([to_section(summed[s, 0], 1, -2 * s) for s in range(experts_n)], axis=0))
        back_up.append(jnp.concatenate([to_section(summed[s, 1], -1, -2 * s) for s in range(experts_n)], axis=0))

    def finish(residual, mix, back):
        pieces = []
        for unit in range(UNITS):
            mixed = jnp.dot(
                mix, back[unit].astype(jnp.float32), precision=lax.Precision.HIGHEST, preferred_element_type=jnp.float32
            )
            pieces += [mixed[:rows_n], mixed[rows_n:]]
        mixed = jnp.concatenate(pieces, axis=1)
        return (residual.astype(jnp.float32) + mixed).astype(jnp.bfloat16)[None]

    return finish(res_down, mix_down, back_down), finish(res_up, mix_up, back_up)


def solution(mesh):
    placed = (
        P("pipe", "expert", None),
        P("pipe", "expert", None),
        P("pipe", "expert", None),
        P("pipe", "expert", None),
        P("pipe", None),
        P("pipe", None, None),
        P("pipe", None, "expert"),
        P("pipe", None, "expert"),
        P("pipe", "expert", None),
    )
    return jax.shard_map(
        on_device,
        mesh=mesh,
        in_specs=placed,
        out_specs=(P("pipe", "expert", None), P("pipe", "expert", None)),
        check_vma=False,
    )
```

```python
import jax
import jax.numpy as jnp
from jax import lax
from jax.sharding import PartitionSpec as P

CAP = 12
ALONG_X = 4

route_scale = 2.5


def index_of(z, x):
    return z * ALONG_X + x


def places():
    columns = lax.axis_size("expert") // ALONG_X
    return [(z, x) for z in range(columns) for x in range(ALONG_X)]


def along_z(block, step):
    columns = lax.axis_size("expert") // ALONG_X
    route = [(index_of(z, x), index_of((z + step) % columns, x)) for z, x in places()]
    return lax.ppermute(block, "expert", route)


def to_section(block, section_step, z_step):
    sections, devices = lax.axis_size("pipe"), lax.axis_size("expert")
    columns = devices // ALONG_X
    route = [
        (
            s * devices + index_of(z, x),
            (s + section_step) % sections * devices + index_of((z + z_step) % columns, x),
        )
        for s in range(sections)
        for z, x in places()
    ]
    return lax.ppermute(block, ("pipe", "expert"), route)


def facing(block, z_flip, x_flip):
    route = [(index_of(z, x), index_of(z ^ z_flip, x ^ x_flip)) for z, x in places()]
    return lax.ppermute(block, "expert", route)


def ring_gather(block):
    columns = lax.axis_size("expert") // ALONG_X
    rings = [[index_of(z, x) for x in range(ALONG_X)] for z in range(columns)]
    return lax.all_gather(block, "expert", axis=0, tiled=True, axis_index_groups=rings)


def prepare(x, routes, gain, router, group):
    xf = x.astype(jnp.float32)
    mean_sq = jnp.mean(xf * xf, axis=-1, keepdims=True)
    normed = (xf * lax.rsqrt(mean_sq + 1e-06) * gain).astype(jnp.bfloat16)
    logits = jnp.dot(normed, router, preferred_element_type=jnp.float32)
    affinity = jax.nn.sigmoid(logits)
    experts_n = router.shape[1]
    hits = routes[:, :, None] == jnp.arange(experts_n, dtype=jnp.int32)
    picked = jnp.sum(jnp.where(hits, affinity[:, None, :], 0.0), axis=2)
    weights = picked / jnp.sum(picked, axis=1, keepdims=True) * route_scale
    named = jnp.any(hits, axis=1)
    share = jnp.sum(jnp.where(hits, weights[:, :, None], 0.0), axis=1)
    count = named.astype(jnp.int32)
    before = jnp.cumsum(count, axis=0) - count
    turn = jnp.mod(jnp.arange(experts_n, dtype=jnp.int32) + group, experts_n)
    rolled = turn[:, None] == jnp.arange(experts_n, dtype=jnp.int32)
    pick = lambda v: jnp.sum(jnp.where(rolled, v[:, None, :], jnp.zeros((), v.dtype)), axis=2)
    slot = jnp.where(pick(count) > 0, pick(before), -1)
    chosen = slot[:, :, None] == jnp.arange(CAP, dtype=jnp.int32)
    combine = jnp.where(chosen, pick(share)[:, :, None], 0.0)
    return normed, chosen, combine


def in_terms(value):
    high = value.astype(jnp.bfloat16)
    rest = value - high.astype(jnp.float32)
    middle = rest.astype(jnp.bfloat16)
    low = (rest - middle.astype(jnp.float32)).astype(jnp.bfloat16)
    return [high, middle, low]


def on_device(act_down, act_up, routes_down, routes_up, norm_gain, router_w, w_gate, w_up, w_down):
    experts_n = router_w.shape[2]
    width = act_down.shape[2]
    rows_n = act_down.shape[1]
    slots = experts_n * CAP
    piece = width // 2
    gain = norm_gain[0]
    router = router_w[0]
    hidden_n = w_down.shape[1]
    place = lax.axis_index("expert")
    group = place // ALONG_X // 2
    column = place % ALONG_X

    both_cols = jnp.concatenate([w_gate[0], w_up[0]], axis=1)
    next_cols = facing(both_cols, 0, 1)
    down_rows = ring_gather(w_down[0])

    normed_d, chosen_d, combine_d = prepare(act_down[0], routes_down[0], gain, router, group)
    normed_u, chosen_u, combine_u = prepare(act_up[0], routes_up[0], gain, router, group)
    select = jnp.stack(
        [jnp.pad(chosen_d, ((0, rows_n), (0, 0), (0, 0))), jnp.pad(chosen_u, ((rows_n, 0), (0, 0), (0, 0)))],
        axis=2,
    ).reshape(2 * rows_n, 2 * slots)
    packed = lax.dot_general(
        select.astype(jnp.bfloat16),
        jnp.concatenate([normed_d, normed_u], axis=0),
        (((0,), (0,)), ((), ())),
        preferred_element_type=jnp.float32,
    ).astype(jnp.bfloat16)

    def ahead(x, combine, step):
        terms = in_terms(combine.reshape(rows_n, slots))
        pad = jnp.zeros((rows_n, -(-3 * slots // 128) * 128 - 3 * slots), jnp.bfloat16)
        sent = to_section(jnp.concatenate([x] + terms + [pad], axis=1), step, 0)
        share = sum(sent[:, width + i * slots:width + (i + 1) * slots].astype(jnp.float32) for i in range(3))
        share = share.reshape(1, rows_n, experts_n, 1, CAP) * jnp.eye(2, dtype=jnp.float32).reshape(2, 1, 1, 2, 1)
        return sent[:, :width], share.reshape(2 * rows_n, 2 * slots)

    res_down, mix_down = ahead(act_down[0], combine_d, 1)
    res_up, mix_up = ahead(act_up[0], combine_u, -1)

    chunk = 2 * CAP
    near = [packed[:chunk]] + [
        along_z(packed[s * chunk:(s + 1) * chunk], 2 * s) for s in range(1, experts_n)
    ]
    mine = jnp.concatenate([c[:CAP] for c in near] + [c[CAP:] for c in near], axis=0)
    mine, res_down, res_up = lax.optimization_barrier((mine, res_down, res_up))
    rows = [mine, facing(mine, 1, 0), facing(mine, 0, 3), facing(mine, 1, 3)]

    dot = lambda a, b: jnp.dot(a, b, preferred_element_type=jnp.float32)
    act = lambda joined: (jax.nn.silu(joined[:, :hidden_n]) * joined[:, hidden_n:]).astype(jnp.bfloat16)
    near_rows = jnp.concatenate(rows[:2], axis=0)
    far_rows = jnp.concatenate(rows[2:], axis=0)
    sent = jnp.concatenate([act(dot(far_rows, both_cols)), act(dot(far_rows, next_cols))], axis=1)
    kept = [act(dot(near_rows, both_cols)), act(dot(near_rows, next_cols))]
    sent, down_rows = lax.optimization_barrier((sent, down_rows))
    got = facing(sent, 0, 3)
    blocks = kept + [got[:, hidden_n:], got[:, :hidden_n]]
    for bit in (1, 2):
        flip = (column & bit) > 0
        blocks = [jnp.where(flip, blocks[i ^ bit], blocks[i]) for i in range(ALONG_X)]
    total = dot(jnp.concatenate(blocks, axis=1), down_rows)

    def send_back(own, theirs, step):
        summed = (own + facing(theirs.astype(jnp.bfloat16), 1, 0).astype(jnp.float32)).astype(jnp.bfloat16)
        summed = summed.reshape(experts_n, CAP, 2, piece).transpose(0, 2, 1, 3).reshape(experts_n, chunk, piece)
        return jnp.concatenate([to_section(summed[s], step, -2 * s) for s in range(experts_n)], axis=0)

    back_down = send_back(total[:slots], total[2 * slots:3 * slots], 1)
    back_up = send_back(total[slots:2 * slots], total[3 * slots:], -1)

    def finish(residual, mix, back):
        mixed = jnp.dot(
            mix, back.astype(jnp.float32), precision=lax.Precision.HIGHEST, preferred_element_type=jnp.float32
        )
        mixed = jnp.concatenate([mixed[:rows_n], mixed[rows_n:]], axis=1)
        return (residual.astype(jnp.float32) + mixed).astype(jnp.bfloat16)[None]

    return finish(res_down, mix_down, back_down), finish(res_up, mix_up, back_up)


def solution(mesh):
    placed = (
        P("pipe", "expert", None),
        P("pipe", "expert", None),
        P("pipe", "expert", None),
        P("pipe", "expert", None),
        P("pipe", None),
        P("pipe", None, None),
        P("pipe", None, "expert"),
        P("pipe", None, "expert"),
        P("pipe", "expert", None),
    )
    return jax.shard_map(
        on_device,
        mesh=mesh,
        in_specs=placed,
        out_specs=(P("pipe", "expert", None), P("pipe", "expert", None)),
        check_vma=False,
    )
```

```python
import jax
import jax.numpy as jnp
from jax import lax
from jax.sharding import PartitionSpec as P

CAP = 12
ALONG_X = 4

route_scale = 2.5


def index_of(z, x):
    return z * ALONG_X + x


def places():
    columns = lax.axis_size("expert") // ALONG_X
    return [(z, x) for z in range(columns) for x in range(ALONG_X)]


def across_groups(chunks):
    pairs = lax.axis_size("expert") // ALONG_X // 2
    members = [[index_of(2 * j + odd, x) for j in range(pairs)] for odd in range(2) for x in range(ALONG_X)]
    return lax.all_to_all(chunks, "expert", split_axis=0, concat_axis=0, tiled=True, axis_index_groups=members)


def across_sections(chunks):
    sections, devices = lax.axis_size("pipe"), lax.axis_size("expert")
    pairs = devices // ALONG_X // 2
    members = [
        [s * devices + index_of(2 * j + odd, x) for s in ((2 * q - 1) % sections, 2 * q) for j in range(pairs)]
        for q in range(sections // 2)
        for odd in range(2)
        for x in range(ALONG_X)
    ]
    return lax.all_to_all(
        chunks, ("pipe", "expert"), split_axis=0, concat_axis=0, tiled=True, axis_index_groups=members
    )


def neighbour(block):
    sections = lax.axis_size("pipe")
    return lax.ppermute(block, "pipe", [(s, (s + 1 if s % 2 else s - 1) % sections) for s in range(sections)])


def same_chip(block):
    return lax.ppermute(block, "pipe", [(s, s ^ 1) for s in range(lax.axis_size("pipe"))])


def facing(block, z_flip, x_flip):
    route = [(index_of(z, x), index_of(z ^ z_flip, x ^ x_flip)) for z, x in places()]
    return lax.ppermute(block, "expert", route)


def ring_gather(block):
    columns = lax.axis_size("expert") // ALONG_X
    rings = [[index_of(z, x) for x in range(ALONG_X)] for z in range(columns)]
    return lax.all_gather(block, "expert", axis=0, tiled=True, axis_index_groups=rings)


def prepare(x, routes, gain, router):
    xf = x.astype(jnp.float32)
    mean_sq = jnp.mean(xf * xf, axis=-1, keepdims=True)
    normed = (xf * lax.rsqrt(mean_sq + 1e-06) * gain).astype(jnp.bfloat16)
    logits = jnp.dot(normed, router, preferred_element_type=jnp.float32)
    affinity = jax.nn.sigmoid(logits)
    experts_n = router.shape[1]
    hits = routes[:, :, None] == jnp.arange(experts_n, dtype=jnp.int32)
    picked = jnp.sum(jnp.where(hits, affinity[:, None, :], 0.0), axis=2)
    weights = picked / jnp.sum(picked, axis=1, keepdims=True) * route_scale
    named = jnp.any(hits, axis=1)
    share = jnp.sum(jnp.where(hits, weights[:, :, None], 0.0), axis=1)
    count = named.astype(jnp.int32)
    before = jnp.cumsum(count, axis=0) - count
    slot = jnp.where(named, before, -1)
    chosen = slot[:, :, None] == jnp.arange(CAP, dtype=jnp.int32)
    combine = jnp.where(chosen, share[:, :, None], 0.0)
    return normed, chosen, combine


def in_terms(value):
    high = value.astype(jnp.bfloat16)
    rest = value - high.astype(jnp.float32)
    middle = rest.astype(jnp.bfloat16)
    low = (rest - middle.astype(jnp.float32)).astype(jnp.bfloat16)
    return [high, middle, low]


def on_device(act_down, act_up, routes_down, routes_up, norm_gain, router_w, w_gate, w_up, w_down):
    experts_n = router_w.shape[2]
    width = act_down.shape[2]
    rows_n = act_down.shape[1]
    slots = experts_n * CAP
    piece = width // 2
    gain = norm_gain[0]
    router = router_w[0]
    hidden_n = w_down.shape[1]
    place = lax.axis_index("expert")
    odd_section = lax.axis_index("pipe") % 2 == 1
    column = place % ALONG_X

    both_cols = jnp.concatenate([w_gate[0], w_up[0]], axis=1)
    next_cols = facing(both_cols, 0, 1)
    down_rows = ring_gather(w_down[0])
    both_cols, act_down, act_up = lax.optimization_barrier((both_cols, act_down, act_up))

    normed_d, chosen_d, combine_d = prepare(act_down[0], routes_down[0], gain, router)
    normed_u, chosen_u, combine_u = prepare(act_up[0], routes_up[0], gain, router)
    select = jnp.stack(
        [jnp.pad(chosen_d, ((0, rows_n), (0, 0), (0, 0))), jnp.pad(chosen_u, ((rows_n, 0), (0, 0), (0, 0)))],
        axis=2,
    ).reshape(2 * rows_n, 2 * slots)
    packed = lax.dot_general(
        select.astype(jnp.bfloat16),
        jnp.concatenate([normed_d, normed_u], axis=0),
        (((0,), (0,)), ((), ())),
        preferred_element_type=jnp.float32,
    ).astype(jnp.bfloat16)

    chunk = 2 * CAP
    mine = across_groups(packed)
    pair = facing(mine, 1, 0)
    across = facing(mine, 0, 3)
    corner = facing(mine, 1, 3)

    dot = lambda a, b: jnp.dot(a, b, preferred_element_type=jnp.float32)
    exact = lambda a, b: jnp.dot(a, b, precision=lax.Precision.HIGHEST, preferred_element_type=jnp.float32)
    act = lambda joined: (jax.nn.silu(joined[:, :hidden_n]) * joined[:, hidden_n:]).astype(jnp.bfloat16)
    terms_d, terms_u = in_terms(combine_d.reshape(rows_n, slots)), in_terms(combine_u.reshape(rows_n, slots))
    pad = jnp.zeros((rows_n, -(-3 * slots // 128) * 128 - 3 * slots), jnp.bfloat16)
    down_set = jnp.concatenate([act_down[0]] + terms_d + [pad], axis=1)
    up_set = jnp.concatenate([act_up[0]] + terms_u + [pad], axis=1)
    home_set = jnp.where(odd_section, up_set, down_set)
    cross_set, pair = lax.optimization_barrier((jnp.where(odd_section, down_set, up_set), pair))
    cross_set = neighbour(cross_set)
    corner, down_rows = lax.optimization_barrier((corner, down_rows))
    near_rows = jnp.concatenate([mine, pair], axis=0)
    far_rows = jnp.concatenate([across, corner], axis=0)
    sent = jnp.concatenate([act(dot(far_rows, both_cols)), act(dot(far_rows, next_cols))], axis=1)
    kept = [act(dot(near_rows, both_cols)), act(dot(near_rows, next_cols))]
    got = facing(sent, 0, 3)
    got, cross_set = lax.optimization_barrier((got, cross_set))
    blocks = kept + [got[:, hidden_n:], got[:, :hidden_n]]
    for bit in (1, 2):
        flip = (column & bit) > 0
        blocks = [jnp.where(flip, blocks[i ^ bit], blocks[i]) for i in range(ALONG_X)]
    hidden = jnp.concatenate(blocks, axis=1)

    total = dot(hidden, down_rows)
    half = 2 * slots
    summed = total[:half] + facing(total[half:].astype(jnp.bfloat16), 1, 0).astype(jnp.float32)

    number = jnp.arange(2 * slots).reshape(experts_n, 2, CAP).transpose(1, 0, 2)[::-1]
    slot_of = jnp.stack([number, number], axis=2)
    pick = (slot_of.reshape(-1)[:, None] == jnp.arange(2 * slots)).reshape(2, experts_n, 2, CAP, 2 * slots)
    side = jnp.arange(2).reshape(1, 1, 2, 1, 1)
    pick = [(pick & (side == h)).reshape(4 * slots, 2 * slots).astype(jnp.bfloat16) for h in (0, 1)]
    summed = summed.astype(jnp.bfloat16)
    halves = (dot(pick[0], summed[:, :piece]) + dot(pick[1], summed[:, piece:])).astype(jnp.bfloat16)
    back = across_sections(halves)
    from_odd, from_even = back[:2 * slots], back[2 * slots:]
    home_back = jnp.where(odd_section, from_odd, from_even)
    cross_back = jnp.where(odd_section, from_even, from_odd)

    def finish(given, back):
        share = given[:, width:width + 3 * slots].astype(jnp.float32).reshape(rows_n, 3, slots)
        share = (share[:, 0] + share[:, 1] + share[:, 2]).reshape(1, rows_n, experts_n, 1, CAP)
        mix = (share * jnp.eye(2, dtype=jnp.float32).reshape(2, 1, 1, 2, 1)).reshape(2 * rows_n, 2 * slots)
        mixed = exact(mix, back.astype(jnp.float32))
        mixed = jnp.concatenate([mixed[:rows_n], mixed[rows_n:]], axis=1)
        return (given[:, :width].astype(jnp.float32) + mixed).astype(jnp.bfloat16)[None]

    came = same_chip(finish(home_set, home_back))
    crossed = finish(cross_set, cross_back)
    return jnp.where(odd_section, came, crossed), jnp.where(odd_section, crossed, came)


def solution(mesh):
    placed = (
        P("pipe", "expert", None),
        P("pipe", "expert", None),
        P("pipe", "expert", None),
        P("pipe", "expert", None),
        P("pipe", None),
        P("pipe", None, None),
        P("pipe", None, "expert"),
        P("pipe", None, "expert"),
        P("pipe", "expert", None),
    )
    return jax.shard_map(
        on_device,
        mesh=mesh,
        in_specs=placed,
        out_specs=(P("pipe", "expert", None), P("pipe", "expert", None)),
        check_vma=False,
    )
```

```python
import jax
import jax.numpy as jnp
from jax import lax
from jax.sharding import PartitionSpec as P

CAP = 12
ALONG_X = 4

route_scale = 2.5


def index_of(z, x):
    return z * ALONG_X + x


def places():
    columns = lax.axis_size("expert") // ALONG_X
    return [(z, x) for z in range(columns) for x in range(ALONG_X)]


def across_groups(chunks):
    pairs = lax.axis_size("expert") // ALONG_X // 2
    members = [[index_of(2 * j + odd, x) for j in range(pairs)] for odd in range(2) for x in range(ALONG_X)]
    return lax.all_to_all(chunks, "expert", split_axis=0, concat_axis=0, tiled=True, axis_index_groups=members)


def across_sections(chunks):
    sections, devices = lax.axis_size("pipe"), lax.axis_size("expert")
    pairs = devices // ALONG_X // 2
    members = [
        [s * devices + index_of(2 * j + odd, x) for s in ((2 * q - 1) % sections, 2 * q) for j in range(pairs)]
        for q in range(sections // 2)
        for odd in range(2)
        for x in range(ALONG_X)
    ]
    return lax.all_to_all(
        chunks, ("pipe", "expert"), split_axis=0, concat_axis=0, tiled=True, axis_index_groups=members
    )


def neighbour(block):
    sections = lax.axis_size("pipe")
    return lax.ppermute(block, "pipe", [(s, (s + 1 if s % 2 else s - 1) % sections) for s in range(sections)])


def facing(block, z_flip, even, odd):
    devices = lax.axis_size("expert")
    route = [
        (s * devices + index_of(z, x), s * devices + index_of(z ^ z_flip, x ^ (odd if s % 2 else even)))
        for s in range(lax.axis_size("pipe"))
        for z, x in places()
    ]
    return lax.ppermute(block, ("pipe", "expert"), route)


def other_core(block, z_flip):
    devices = lax.axis_size("expert")
    route = [
        (s * devices + index_of(z, x), (s ^ 1) * devices + index_of(z ^ z_flip, x))
        for s in range(lax.axis_size("pipe"))
        for z, x in places()
    ]
    return lax.ppermute(block, ("pipe", "expert"), route)


def ring_gather(block):
    columns = lax.axis_size("expert") // ALONG_X
    rings = [[index_of(z, x) for x in range(ALONG_X)] for z in range(columns)]
    return lax.all_gather(block, "expert", axis=0, tiled=True, axis_index_groups=rings)


def prepare(x, routes, gain, router):
    xf = x.astype(jnp.float32)
    mean_sq = jnp.mean(xf * xf, axis=-1, keepdims=True)
    normed = (xf * lax.rsqrt(mean_sq + 1e-06) * gain).astype(jnp.bfloat16)
    logits = jnp.dot(normed, router, preferred_element_type=jnp.float32)
    affinity = jax.nn.sigmoid(logits)
    experts_n = router.shape[1]
    hits = routes[:, :, None] == jnp.arange(experts_n, dtype=jnp.int32)
    picked = jnp.sum(jnp.where(hits, affinity[:, None, :], 0.0), axis=2)
    weights = picked / jnp.sum(picked, axis=1, keepdims=True) * route_scale
    named = jnp.any(hits, axis=1)
    share = jnp.sum(jnp.where(hits, weights[:, :, None], 0.0), axis=1)
    count = named.astype(jnp.int32)
    before = jnp.cumsum(count, axis=0) - count
    slot = jnp.where(named, before, -1)
    chosen = slot[:, :, None] == jnp.arange(CAP, dtype=jnp.int32)
    combine = jnp.where(chosen, share[:, :, None], 0.0)
    return normed, chosen, combine


def in_terms(value):
    high = value.astype(jnp.bfloat16)
    rest = value - high.astype(jnp.float32)
    middle = rest.astype(jnp.bfloat16)
    low = (rest - middle.astype(jnp.float32)).astype(jnp.bfloat16)
    return [high, middle, low]


def on_device(act_down, act_up, routes_down, routes_up, norm_gain, router_w, w_gate, w_up, w_down):
    experts_n = router_w.shape[2]
    width = act_down.shape[2]
    rows_n = act_down.shape[1]
    slots = experts_n * CAP
    piece = width // 2
    gain = norm_gain[0]
    router = router_w[0]
    hidden_n = w_down.shape[1]
    place = lax.axis_index("expert")
    odd_section = lax.axis_index("pipe") % 2 == 1
    column = place % ALONG_X

    both_cols = jnp.concatenate([w_gate[0], w_up[0]], axis=1)
    next_cols = facing(both_cols, 0, 1, 3)
    down_rows = ring_gather(w_down[0])
    both_cols, act_down, act_up = lax.optimization_barrier((both_cols, act_down, act_up))

    normed_d, chosen_d, combine_d = prepare(act_down[0], routes_down[0], gain, router)
    normed_u, chosen_u, combine_u = prepare(act_up[0], routes_up[0], gain, router)
    select = jnp.stack(
        [jnp.pad(chosen_d, ((0, rows_n), (0, 0), (0, 0))), jnp.pad(chosen_u, ((rows_n, 0), (0, 0), (0, 0)))],
        axis=2,
    ).reshape(2 * rows_n, 2 * slots)
    packed = lax.dot_general(
        select.astype(jnp.bfloat16),
        jnp.concatenate([normed_d, normed_u], axis=0),
        (((0,), (0,)), ((), ())),
        preferred_element_type=jnp.float32,
    ).astype(jnp.bfloat16)

    chunk = 2 * CAP
    terms_d, terms_u = in_terms(combine_d.reshape(rows_n, slots)), in_terms(combine_u.reshape(rows_n, slots))
    pad = jnp.zeros((rows_n, -(-3 * slots // 128) * 128 - 3 * slots), jnp.bfloat16)
    down_set = jnp.concatenate([act_down[0]] + terms_d + [pad], axis=1)
    up_set = jnp.concatenate([act_up[0]] + terms_u + [pad], axis=1)
    home_set, cross_set = jnp.where(odd_section, up_set, down_set), jnp.where(odd_section, down_set, up_set)
    home_set = other_core(home_set, 0)
    mine = across_groups(packed)
    mine, home_set = lax.optimization_barrier((mine, home_set))
    pair = facing(mine, 1, 0, 0)
    across = facing(mine, 0, 3, 1)
    corner = facing(mine, 1, 3, 1)

    dot = lambda a, b: jnp.dot(a, b, preferred_element_type=jnp.float32)
    exact = lambda a, b: jnp.dot(a, b, precision=lax.Precision.HIGHEST, preferred_element_type=jnp.float32)
    act = lambda joined: (jax.nn.silu(joined[:, :hidden_n]) * joined[:, hidden_n:]).astype(jnp.bfloat16)
    cross_set, pair = lax.optimization_barrier((cross_set, pair))
    cross_set = neighbour(cross_set)
    corner, down_rows = lax.optimization_barrier((corner, down_rows))
    near_rows = jnp.concatenate([mine, pair], axis=0)
    far_rows = jnp.concatenate([across, corner], axis=0)
    sent = jnp.concatenate([act(dot(far_rows, both_cols)), act(dot(far_rows, next_cols))], axis=1)
    kept = [act(dot(near_rows, both_cols)), act(dot(near_rows, next_cols))]
    got = facing(sent, 0, 3, 1)
    got, cross_set = lax.optimization_barrier((got, cross_set))
    first, second = got[:, :hidden_n], got[:, hidden_n:]
    one, three = jnp.where(odd_section, first, kept[1]), jnp.where(odd_section, kept[1], first)
    blocks = [kept[0], one, second, three]
    for bit in (1, 2):
        flip = (column & bit) > 0
        blocks = [jnp.where(flip, blocks[i ^ bit], blocks[i]) for i in range(ALONG_X)]
    hidden = jnp.concatenate(blocks, axis=1)

    batch = jnp.arange(2).reshape(1, 2, 1, 1) ^ odd_section.astype(jnp.int32)
    row_of = lambda owner: (owner * experts_n + jnp.arange(experts_n).reshape(1, 1, -1, 1)) * chunk
    row_of = row_of(jnp.arange(2).reshape(2, 1, 1, 1)[::-1]) + batch * CAP + jnp.arange(CAP)
    order = (row_of.reshape(-1)[:, None] == jnp.arange(4 * slots)).astype(jnp.bfloat16)
    hidden = dot(order, hidden).astype(jnp.bfloat16)
    away = dot(hidden[:2 * slots], down_rows).astype(jnp.bfloat16)
    home, cross = other_core(away[:slots], 1), facing(away[slots:], 1, 0, 0)
    stays = dot(hidden[2 * slots:], down_rows)
    home = home.astype(jnp.float32) + other_core(stays[:slots].astype(jnp.bfloat16), 0).astype(jnp.float32)
    cross = cross.astype(jnp.float32) + stays[slots:]
    summed = jnp.concatenate([home, cross], axis=0).astype(jnp.bfloat16)

    source = jnp.arange(2).reshape(2, 1, 1, 1, 1) ^ 1 ^ odd_section.astype(jnp.int32)
    slot_of = source * slots + jnp.arange(experts_n).reshape(1, -1, 1, 1, 1) * CAP
    slot_of = slot_of + jnp.arange(CAP).reshape(1, 1, 1, CAP, 1) == jnp.arange(2 * slots)
    side = jnp.arange(2).reshape(1, 1, 2, 1, 1)
    pick = [(slot_of & (side == h)).reshape(4 * slots, 2 * slots).astype(jnp.bfloat16) for h in (0, 1)]
    halves = (dot(pick[0], summed[:, :piece]) + dot(pick[1], summed[:, piece:])).astype(jnp.bfloat16)
    back = across_sections(halves)

    def finish(given, back):
        share = given[:, width:width + 3 * slots].astype(jnp.float32).reshape(rows_n, 3, slots)
        share = (share[:, 0] + share[:, 1] + share[:, 2]).reshape(1, rows_n, experts_n, 1, CAP)
        mix = (share * jnp.eye(2, dtype=jnp.float32).reshape(2, 1, 1, 2, 1)).reshape(2 * rows_n, 2 * slots)
        mixed = exact(mix, back.astype(jnp.float32))
        mixed = jnp.concatenate([mixed[:rows_n], mixed[rows_n:]], axis=1)
        return (given[:, :width].astype(jnp.float32) + mixed).astype(jnp.bfloat16)[None]

    down_set, up_set = jnp.where(odd_section, home_set, cross_set), jnp.where(odd_section, cross_set, home_set)
    return finish(down_set, back[:2 * slots]), finish(up_set, back[2 * slots:])


def solution(mesh):
    placed = (
        P("pipe", "expert", None),
        P("pipe", "expert", None),
        P("pipe", "expert", None),
        P("pipe", "expert", None),
        P("pipe", None),
        P("pipe", None, None),
        P("pipe", None, "expert"),
        P("pipe", None, "expert"),
        P("pipe", "expert", None),
    )
    return jax.shard_map(
        on_device,
        mesh=mesh,
        in_specs=placed,
        out_specs=(P("pipe", "expert", None), P("pipe", "expert", None)),
        check_vma=False,
    )
```

```python
import jax
import jax.numpy as jnp
from jax import lax
from jax.sharding import PartitionSpec as P

CAP = 12
ALONG_X = 4

route_scale = 2.5


def index_of(z, x):
    return z * ALONG_X + x


def places():
    columns = lax.axis_size("expert") // ALONG_X
    return [(z, x) for z in range(columns) for x in range(ALONG_X)]


def across_groups(chunks):
    pairs = lax.axis_size("expert") // ALONG_X // 2
    members = [[index_of(2 * j + odd, x) for j in range(pairs)] for odd in range(2) for x in range(ALONG_X)]
    return lax.all_to_all(chunks, "expert", split_axis=0, concat_axis=0, tiled=True, axis_index_groups=members)


def across_sections(chunks):
    sections, devices = lax.axis_size("pipe"), lax.axis_size("expert")
    pairs = devices // ALONG_X // 2
    members = [
        [s * devices + index_of(2 * j + odd, x) for s in ((2 * q - 1) % sections, 2 * q) for j in range(pairs)]
        for q in range(sections // 2)
        for odd in range(2)
        for x in range(ALONG_X)
    ]
    return lax.all_to_all(
        chunks, ("pipe", "expert"), split_axis=0, concat_axis=0, tiled=True, axis_index_groups=members
    )


def neighbour(block):
    sections = lax.axis_size("pipe")
    return lax.ppermute(block, "pipe", [(s, (s + 1 if s % 2 else s - 1) % sections) for s in range(sections)])


def facing(block, z_flip, even, odd):
    devices = lax.axis_size("expert")
    route = [
        (s * devices + index_of(z, x), s * devices + index_of(z ^ z_flip, x ^ (odd if s % 2 else even)))
        for s in range(lax.axis_size("pipe"))
        for z, x in places()
    ]
    return lax.ppermute(block, ("pipe", "expert"), route)


def other_core(block, z_flip):
    devices = lax.axis_size("expert")
    route = [
        (s * devices + index_of(z, x), (s ^ 1) * devices + index_of(z ^ z_flip, x))
        for s in range(lax.axis_size("pipe"))
        for z, x in places()
    ]
    return lax.ppermute(block, ("pipe", "expert"), route)


def ring_gather(block):
    columns = lax.axis_size("expert") // ALONG_X
    rings = [[index_of(z, x) for x in range(ALONG_X)] for z in range(columns)]
    return lax.all_gather(block, "expert", axis=0, tiled=True, axis_index_groups=rings)


def prepare(x, routes, gain, router):
    xf = x.astype(jnp.float32)
    mean_sq = jnp.mean(xf * xf, axis=-1, keepdims=True)
    normed = (xf * lax.rsqrt(mean_sq + 1e-06) * gain).astype(jnp.bfloat16)
    logits = jnp.dot(normed, router, preferred_element_type=jnp.float32)
    affinity = jax.nn.sigmoid(logits)
    experts_n = router.shape[1]
    hits = routes[:, :, None] == jnp.arange(experts_n, dtype=jnp.int32)
    picked = jnp.sum(jnp.where(hits, affinity[:, None, :], 0.0), axis=2)
    weights = picked / jnp.sum(picked, axis=1, keepdims=True) * route_scale
    named = jnp.any(hits, axis=1)
    share = jnp.sum(jnp.where(hits, weights[:, :, None], 0.0), axis=1)
    count = named.astype(jnp.int32)
    before = jnp.cumsum(count, axis=0) - count
    slot = jnp.where(named, before, -1)
    chosen = slot[:, :, None] == jnp.arange(CAP, dtype=jnp.int32)
    combine = jnp.where(chosen, share[:, :, None], 0.0)
    return normed, chosen, combine


def in_terms(value):
    high = value.astype(jnp.bfloat16)
    rest = value - high.astype(jnp.float32)
    middle = rest.astype(jnp.bfloat16)
    low = (rest - middle.astype(jnp.float32)).astype(jnp.bfloat16)
    return [high, middle, low]


def on_device(act_down, act_up, routes_down, routes_up, norm_gain, router_w, w_gate, w_up, w_down):
    experts_n = router_w.shape[2]
    width = act_down.shape[2]
    rows_n = act_down.shape[1]
    slots = experts_n * CAP
    piece = width // 2
    gain = norm_gain[0]
    router = router_w[0]
    hidden_n = w_down.shape[1]
    place = lax.axis_index("expert")
    odd_section = lax.axis_index("pipe") % 2 == 1
    column = place % ALONG_X

    both_cols = jnp.concatenate([w_gate[0], w_up[0]], axis=1)
    next_cols = facing(both_cols, 0, 1, 3)
    down_rows = ring_gather(w_down[0])
    both_cols, act_down, act_up = lax.optimization_barrier((both_cols, act_down, act_up))

    normed_d, chosen_d, combine_d = prepare(act_down[0], routes_down[0], gain, router)
    normed_u, chosen_u, combine_u = prepare(act_up[0], routes_up[0], gain, router)
    select = jnp.stack(
        [jnp.pad(chosen_d, ((0, rows_n), (0, 0), (0, 0))), jnp.pad(chosen_u, ((rows_n, 0), (0, 0), (0, 0)))],
        axis=2,
    ).reshape(2 * rows_n, 2 * slots)
    packed = lax.dot_general(
        select.astype(jnp.bfloat16),
        jnp.concatenate([normed_d, normed_u], axis=0),
        (((0,), (0,)), ((), ())),
        preferred_element_type=jnp.float32,
    ).astype(jnp.bfloat16)

    chunk = 2 * CAP
    terms_d, terms_u = in_terms(combine_d.reshape(rows_n, slots)), in_terms(combine_u.reshape(rows_n, slots))
    pad = jnp.zeros((rows_n, -(-3 * slots // 128) * 128 - 3 * slots), jnp.bfloat16)
    down_set = jnp.concatenate([act_down[0]] + terms_d + [pad], axis=1)
    up_set = jnp.concatenate([act_up[0]] + terms_u + [pad], axis=1)
    home_set, cross_set = jnp.where(odd_section, up_set, down_set), jnp.where(odd_section, down_set, up_set)
    home_set = other_core(home_set, 0)
    mine = across_groups(packed)
    mine, home_set = lax.optimization_barrier((mine, home_set))
    pair = facing(mine, 1, 0, 0)
    across = facing(mine, 0, 3, 1)
    corner = facing(mine, 1, 3, 1)

    dot = lambda a, b: jnp.dot(a, b, preferred_element_type=jnp.float32)
    exact = lambda a, b: jnp.dot(a, b, precision=lax.Precision.HIGHEST, preferred_element_type=jnp.float32)
    all_cols = jnp.concatenate([both_cols, next_cols], axis=1)
    cross_set, all_cols, pair = lax.optimization_barrier((cross_set, all_cols, pair))
    cross_set = neighbour(cross_set)
    corner, down_rows = lax.optimization_barrier((corner, down_rows))
    near_rows = jnp.concatenate([mine, pair], axis=0)
    far_rows = jnp.concatenate([across, corner], axis=0)
    def units(rows):
        joined = dot(rows, all_cols).reshape(rows.shape[0], 2, 2 * hidden_n)
        return (jax.nn.silu(joined[:, :, :hidden_n]) * joined[:, :, hidden_n:]).astype(jnp.bfloat16)

    sent = units(far_rows).reshape(4 * slots, 2 * hidden_n)
    kept = units(near_rows)
    kept = [kept[:, 0], kept[:, 1]]
    got = facing(sent, 0, 3, 1)
    got, cross_set = lax.optimization_barrier((got, cross_set))
    first, second = got[:, :hidden_n], got[:, hidden_n:]
    one, three = jnp.where(odd_section, first, kept[1]), jnp.where(odd_section, kept[1], first)
    blocks = [kept[0], one, second, three]
    for bit in (1, 2):
        flip = (column & bit) > 0
        blocks = [jnp.where(flip, blocks[i ^ bit], blocks[i]) for i in range(ALONG_X)]
    hidden = jnp.concatenate(blocks, axis=1)

    batch = jnp.arange(2).reshape(1, 2, 1, 1) ^ odd_section.astype(jnp.int32)
    row_of = lambda owner: (owner * experts_n + jnp.arange(experts_n).reshape(1, 1, -1, 1)) * chunk
    row_of = row_of(jnp.arange(2).reshape(2, 1, 1, 1)[::-1]) + batch * CAP + jnp.arange(CAP)
    order = (row_of.reshape(-1)[:, None] == jnp.arange(4 * slots)).astype(jnp.bfloat16)
    hidden = dot(order, hidden).astype(jnp.bfloat16)
    away = dot(hidden[:2 * slots], down_rows).astype(jnp.bfloat16)
    home, cross = other_core(away[:slots], 1), facing(away[slots:], 1, 0, 0)
    stays = dot(hidden[2 * slots:], down_rows)
    home = home.astype(jnp.float32) + other_core(stays[:slots].astype(jnp.bfloat16), 0).astype(jnp.float32)
    cross = cross.astype(jnp.float32) + stays[slots:]
    summed = jnp.concatenate([home, cross], axis=0).astype(jnp.bfloat16)

    source = jnp.arange(2).reshape(2, 1, 1, 1, 1) ^ 1 ^ odd_section.astype(jnp.int32)
    slot_of = source * slots + jnp.arange(experts_n).reshape(1, -1, 1, 1, 1) * CAP
    slot_of = slot_of + jnp.arange(CAP).reshape(1, 1, 1, CAP, 1) == jnp.arange(2 * slots)
    side = jnp.arange(2).reshape(1, 1, 2, 1, 1)
    pick = [(slot_of & (side == h)).reshape(4 * slots, 2 * slots).astype(jnp.bfloat16) for h in (0, 1)]
    halves = (dot(pick[0], summed[:, :piece]) + dot(pick[1], summed[:, piece:])).astype(jnp.bfloat16)
    back = across_sections(halves)

    def finish(given, back):
        share = given[:, width:width + 3 * slots].astype(jnp.float32).reshape(rows_n, 3, slots)
        share = (share[:, 0] + share[:, 1] + share[:, 2]).reshape(1, rows_n, experts_n, 1, CAP)
        mix = (share * jnp.eye(2, dtype=jnp.float32).reshape(2, 1, 1, 2, 1)).reshape(2 * rows_n, 2 * slots)
        mixed = exact(mix, back.astype(jnp.float32))
        mixed = jnp.concatenate([mixed[:rows_n], mixed[rows_n:]], axis=1)
        return (given[:, :width].astype(jnp.float32) + mixed).astype(jnp.bfloat16)[None]

    down_set, up_set = jnp.where(odd_section, home_set, cross_set), jnp.where(odd_section, cross_set, home_set)
    return finish(down_set, back[:2 * slots]), finish(up_set, back[2 * slots:])


def solution(mesh):
    placed = (
        P("pipe", "expert", None),
        P("pipe", "expert", None),
        P("pipe", "expert", None),
        P("pipe", "expert", None),
        P("pipe", None),
        P("pipe", None, None),
        P("pipe", None, "expert"),
        P("pipe", None, "expert"),
        P("pipe", "expert", None),
    )
    return jax.shard_map(
        on_device,
        mesh=mesh,
        in_specs=placed,
        out_specs=(P("pipe", "expert", None), P("pipe", "expert", None)),
        check_vma=False,
    )
```

```python
import jax
import jax.numpy as jnp
from jax import lax
from jax.sharding import PartitionSpec as P

CAP = 12
ALONG_X = 4

route_scale = 2.5


def index_of(z, x):
    return z * ALONG_X + x


def places():
    columns = lax.axis_size("expert") // ALONG_X
    return [(z, x) for z in range(columns) for x in range(ALONG_X)]


def across_groups(chunks):
    pairs = lax.axis_size("expert") // ALONG_X // 2
    members = [[index_of(2 * j + odd, x) for j in range(pairs)] for odd in range(2) for x in range(ALONG_X)]
    return lax.all_to_all(chunks, "expert", split_axis=0, concat_axis=0, tiled=True, axis_index_groups=members)


def across_sections(chunks):
    sections, devices = lax.axis_size("pipe"), lax.axis_size("expert")
    pairs = devices // ALONG_X // 2
    members = [
        [s * devices + index_of(2 * j + odd, x) for s in ((2 * q - 1) % sections, 2 * q) for j in range(pairs)]
        for q in range(sections // 2)
        for odd in range(2)
        for x in range(ALONG_X)
    ]
    return lax.all_to_all(
        chunks, ("pipe", "expert"), split_axis=0, concat_axis=0, tiled=True, axis_index_groups=members
    )


def neighbour(block):
    sections = lax.axis_size("pipe")
    return lax.ppermute(block, "pipe", [(s, (s + 1 if s % 2 else s - 1) % sections) for s in range(sections)])


def facing(block, z_flip, even, odd):
    devices = lax.axis_size("expert")
    route = [
        (s * devices + index_of(z, x), s * devices + index_of(z ^ z_flip, x ^ (odd if s % 2 else even)))
        for s in range(lax.axis_size("pipe"))
        for z, x in places()
    ]
    return lax.ppermute(block, ("pipe", "expert"), route)


def other_core(block, z_flip):
    devices = lax.axis_size("expert")
    route = [
        (s * devices + index_of(z, x), (s ^ 1) * devices + index_of(z ^ z_flip, x))
        for s in range(lax.axis_size("pipe"))
        for z, x in places()
    ]
    return lax.ppermute(block, ("pipe", "expert"), route)


def ring_gather(block):
    columns = lax.axis_size("expert") // ALONG_X
    rings = [[index_of(z, x) for x in range(ALONG_X)] for z in range(columns)]
    return lax.all_gather(block, "expert", axis=0, tiled=True, axis_index_groups=rings)


def prepare(x, routes, gain, router):
    xf = x.astype(jnp.float32)
    mean_sq = jnp.mean(xf * xf, axis=-1, keepdims=True)
    normed = (xf * lax.rsqrt(mean_sq + 1e-06) * gain).astype(jnp.bfloat16)
    logits = jnp.dot(normed, router, preferred_element_type=jnp.float32)
    affinity = jax.nn.sigmoid(logits)
    experts_n = router.shape[1]
    hits = routes[:, :, None] == jnp.arange(experts_n, dtype=jnp.int32)
    picked = jnp.sum(jnp.where(hits, affinity[:, None, :], 0.0), axis=2)
    weights = picked / jnp.sum(picked, axis=1, keepdims=True) * route_scale
    named = jnp.any(hits, axis=1)
    share = jnp.sum(jnp.where(hits, weights[:, :, None], 0.0), axis=1)
    count = named.astype(jnp.int32)
    before = jnp.cumsum(count, axis=0) - count
    slot = jnp.where(named, before, -1)
    chosen = slot[:, :, None] == jnp.arange(CAP, dtype=jnp.int32)
    combine = jnp.where(chosen, share[:, :, None], 0.0)
    return normed, chosen, combine


def in_terms(value):
    rounded = lambda v: lax.reduce_precision(v, exponent_bits=8, mantissa_bits=7)
    high = rounded(value)
    middle = rounded(value - high)
    low = rounded(value - high - middle)
    return [term.astype(jnp.bfloat16) for term in (high, middle, low)]


def on_device(act_down, act_up, routes_down, routes_up, norm_gain, router_w, w_gate, w_up, w_down):
    experts_n = router_w.shape[2]
    width = act_down.shape[2]
    rows_n = act_down.shape[1]
    slots = experts_n * CAP
    piece = width // 2
    gain = norm_gain[0]
    router = router_w[0]
    hidden_n = w_down.shape[1]
    place = lax.axis_index("expert")
    odd_section = lax.axis_index("pipe") % 2 == 1
    column = place % ALONG_X

    both_cols = jnp.concatenate([w_gate[0], w_up[0]], axis=1)
    next_cols = facing(both_cols, 0, 1, 3)
    down_rows = ring_gather(w_down[0])
    both_cols, act_down, act_up = lax.optimization_barrier((both_cols, act_down, act_up))

    normed_d, chosen_d, combine_d = prepare(act_down[0], routes_down[0], gain, router)
    normed_u, chosen_u, combine_u = prepare(act_up[0], routes_up[0], gain, router)
    select = jnp.stack(
        [jnp.pad(chosen_d, ((0, rows_n), (0, 0), (0, 0))), jnp.pad(chosen_u, ((rows_n, 0), (0, 0), (0, 0)))],
        axis=2,
    ).reshape(2 * rows_n, 2 * slots)
    packed = lax.dot_general(
        select.astype(jnp.bfloat16),
        jnp.concatenate([normed_d, normed_u], axis=0),
        (((0,), (0,)), ((), ())),
        preferred_element_type=jnp.float32,
    ).astype(jnp.bfloat16)

    chunk = 2 * CAP
    terms_d, terms_u = in_terms(combine_d.reshape(rows_n, slots)), in_terms(combine_u.reshape(rows_n, slots))
    pad = jnp.zeros((rows_n, -(-3 * slots // 128) * 128 - 3 * slots), jnp.bfloat16)
    down_set = jnp.concatenate([act_down[0]] + terms_d + [pad], axis=1)
    up_set = jnp.concatenate([act_up[0]] + terms_u + [pad], axis=1)
    home_set, cross_set = jnp.where(odd_section, up_set, down_set), jnp.where(odd_section, down_set, up_set)
    home_set = other_core(home_set, 0)
    mine = across_groups(packed)
    mine, home_set = lax.optimization_barrier((mine, home_set))
    pair = facing(mine, 1, 0, 0)
    across = facing(mine, 0, 3, 1)
    corner = facing(mine, 1, 3, 1)

    dot = lambda a, b: jnp.dot(a, b, preferred_element_type=jnp.float32)
    exact = lambda a, b: jnp.dot(a, b, precision=lax.Precision.HIGHEST, preferred_element_type=jnp.float32)
    all_cols = jnp.concatenate([both_cols, next_cols], axis=1)
    cross_set, all_cols, pair = lax.optimization_barrier((cross_set, all_cols, pair))
    cross_set = neighbour(cross_set)
    corner, down_rows = lax.optimization_barrier((corner, down_rows))
    near_rows = jnp.concatenate([mine, pair], axis=0)
    far_rows = jnp.concatenate([across, corner], axis=0)
    def units(rows):
        joined = dot(rows, all_cols).reshape(rows.shape[0], 2, 2 * hidden_n)
        return (jax.nn.silu(joined[:, :, :hidden_n]) * joined[:, :, hidden_n:]).astype(jnp.bfloat16)

    sent = units(far_rows).reshape(4 * slots, 2 * hidden_n)
    kept = units(near_rows)
    kept = [kept[:, 0], kept[:, 1]]
    got = facing(sent, 0, 3, 1)
    got, cross_set = lax.optimization_barrier((got, cross_set))
    first, second = got[:, :hidden_n], got[:, hidden_n:]
    one, three = jnp.where(odd_section, first, kept[1]), jnp.where(odd_section, kept[1], first)
    blocks = [kept[0], one, second, three]
    for bit in (1, 2):
        flip = (column & bit) > 0
        blocks = [jnp.where(flip, blocks[i ^ bit], blocks[i]) for i in range(ALONG_X)]
    hidden = jnp.concatenate(blocks, axis=1)

    batch = jnp.arange(2).reshape(1, 2, 1, 1) ^ odd_section.astype(jnp.int32)
    row_of = lambda owner: (owner * experts_n + jnp.arange(experts_n).reshape(1, 1, -1, 1)) * chunk
    row_of = row_of(jnp.arange(2).reshape(2, 1, 1, 1)[::-1]) + batch * CAP + jnp.arange(CAP)
    order = (row_of.reshape(-1)[:, None] == jnp.arange(4 * slots)).astype(jnp.bfloat16)
    hidden = dot(order, hidden).astype(jnp.bfloat16)
    away = dot(hidden[:2 * slots], down_rows).astype(jnp.bfloat16)
    home, cross = other_core(away[:slots], 1), facing(away[slots:], 1, 0, 0)
    stays = dot(hidden[2 * slots:], down_rows)
    home = home.astype(jnp.float32) + other_core(stays[:slots].astype(jnp.bfloat16), 0).astype(jnp.float32)
    cross = cross.astype(jnp.float32) + stays[slots:]
    summed = jnp.concatenate([home, cross], axis=0).astype(jnp.bfloat16)

    source = jnp.arange(2).reshape(2, 1, 1, 1, 1) ^ 1 ^ odd_section.astype(jnp.int32)
    slot_of = source * slots + jnp.arange(experts_n).reshape(1, -1, 1, 1, 1) * CAP
    slot_of = slot_of + jnp.arange(CAP).reshape(1, 1, 1, CAP, 1) == jnp.arange(2 * slots)
    side = jnp.arange(2).reshape(1, 1, 2, 1, 1)
    pick = [(slot_of & (side == h)).reshape(4 * slots, 2 * slots).astype(jnp.bfloat16) for h in (0, 1)]
    halves = (dot(pick[0], summed[:, :piece]) + dot(pick[1], summed[:, piece:])).astype(jnp.bfloat16)
    back = across_sections(halves)

    def finish(given, back):
        share = given[:, width:width + 3 * slots].astype(jnp.float32).reshape(rows_n, 3, slots)
        share = (share[:, 0] + share[:, 1] + share[:, 2]).reshape(1, rows_n, experts_n, 1, CAP)
        mix = (share * jnp.eye(2, dtype=jnp.float32).reshape(2, 1, 1, 2, 1)).reshape(2 * rows_n, 2 * slots)
        mixed = exact(mix, back.astype(jnp.float32))
        mixed = jnp.concatenate([mixed[:rows_n], mixed[rows_n:]], axis=1)
        return (given[:, :width].astype(jnp.float32) + mixed).astype(jnp.bfloat16)[None]

    down_set, up_set = jnp.where(odd_section, home_set, cross_set), jnp.where(odd_section, cross_set, home_set)
    return finish(down_set, back[:2 * slots]), finish(up_set, back[2 * slots:])


def solution(mesh):
    placed = (
        P("pipe", "expert", None),
        P("pipe", "expert", None),
        P("pipe", "expert", None),
        P("pipe", "expert", None),
        P("pipe", None),
        P("pipe", None, None),
        P("pipe", None, "expert"),
        P("pipe", None, "expert"),
        P("pipe", "expert", None),
    )
    return jax.shard_map(
        on_device,
        mesh=mesh,
        in_specs=placed,
        out_specs=(P("pipe", "expert", None), P("pipe", "expert", None)),
        check_vma=False,
    )
```
